32 devices in a mesh: row: 4 (over x, core), col: 4 (over z), dep: 2 (over y).
Axes of the slice: x: 2, y: 2, z: 4, core: 2. Of those that a mesh axis runs over, the one named last changes fastest.
Arguments:
- inputs: bfloat16 [2048, 6144], P(('row', 'dep'), 'col'), may hold values from -6 to 6
- weight: bfloat16 [6144, 24576], P(('col', 'row'), 'dep'), may hold values from -0.078125 to 0.078125
- grad_out: bfloat16 [2048, 24576], P(('row', 'col'), 'dep'), may hold values from -6 to 6
Outputs:
- hidden: bfloat16 [2048, 24576], P(('row', 'col'), 'dep')
- grad_inputs: bfloat16 [2048, 6144], P(('row', 'dep'), 'col')
The draws below stay inside these ranges and needn't reach their ends.
All inputs are finite; a program needn't handle non-finite values.
Results may differ from the reference program's by a relative error of at most 0.022.
Values may be sent and summed in bfloat16 or wider, within the bound.
No kernel may reach another device: no remote copies, remote signals or barrier semaphores. Data moves between devices by JAX's collectives and lax.ppermute only.
A program may use at most 128 MiB of HBM per device.

```python
import jax
import jax.numpy as jnp
from jax import lax

D = 6144
FF = 24576
TOKENS = 2048
N_COL = 4
N_DEP = 2


def strengthened(result, stream_key, source, target, shards_of, factor):
    def block_of(dim):
        return (jnp.arange(result.shape[dim]) // (result.shape[dim] // shards_of)).reshape((-1,) + (1,) * (result.ndim - 1 - dim))

    near = jax.random.permutation(stream_key, shards_of)[block_of(target)]
    second = (block_of(target) + shards_of // 2) % shards_of
    return jnp.where((block_of(source) == near) | (block_of(source) == second), factor * result, result)


def level_of(own_key, dims, cuts, low, largest):
    factor_of = 1.0
    for dim, shards_of in cuts:
        draws = jax.random.uniform(jax.random.fold_in(jax.random.fold_in(own_key, 6), dim), (shards_of,), jnp.float32, low / len(cuts), largest / len(cuts))
        factor_of = factor_of * jnp.repeat(jnp.exp(draws), dims[dim] // shards_of).reshape((-1,) + (1,) * (len(dims) - 1 - dim))
    return factor_of


def centred(rng, dims, spread, bound, split=(), kind=jnp.bfloat16):
    drawn = spread * jax.random.normal(rng, dims, jnp.float32)
    if split:
        drawn = drawn * level_of(rng, dims, split, -0.22, 0.18)
    return jnp.clip(drawn, -bound, bound).astype(kind)


def gaussian_with(key, dims, width, limit, pieces, heavy, kind=jnp.bfloat16):
    array = width * jax.random.normal(key, dims, jnp.float32)
    if pieces:
        array = array * level_of(key, dims, pieces, -0.22, 0.18)
    return jnp.clip(strengthened(array, jax.random.fold_in(key, 3), *heavy), -limit, limit).astype(kind)


def setup_inputs(seed: int = 0) -> dict:
    streams_of = jax.random.split(jax.random.key(seed), 4)
    return {
        "inputs": gaussian_with(streams_of[0], (TOKENS, D), 1.0, 6.0, ((0, 8), (1, 4)), (1, 0, 8, 2.0)),
        "weight": centred(streams_of[1], (D, FF), D ** -0.5, 0.078125, ((0, 16), (1, 2))),
        "grad_out": gaussian_with(streams_of[2], (TOKENS, FF), 1.0, 6.0, ((0, 16), (1, 2)), (1, 0, 16, 2.0)),
    }


def gelu_tanh(values):
    return jax.nn.gelu(values, approximate=True)

def reference(inputs, weight, grad_out):
    width_block = D // N_COL
    hidden_block = FF // N_DEP

    def fwd_term(running, position):
        columns = lax.dynamic_slice_in_dim(inputs, position * width_block, width_block, 1)
        row_block = lax.dynamic_slice_in_dim(weight, position * width_block, width_block, 0)
        product = jnp.dot(columns, row_block, preferred_element_type=jnp.float32).astype(jnp.bfloat16)
        product = lax.optimization_barrier(product).astype(jnp.float32)
        return (running + product, None)
    pre_act, _ = lax.scan(fwd_term, jnp.zeros((TOKENS, FF), jnp.float32), jnp.arange(N_COL, dtype=jnp.int32))
    activation, pullback = jax.vjp(gelu_tanh, pre_act)
    hidden = activation.astype(jnp.bfloat16)
    grad_pre = pullback(grad_out.astype(jnp.float32))[0].astype(jnp.bfloat16)

    def bwd_term(running, position):
        grad_cols = lax.dynamic_slice_in_dim(grad_pre, position * hidden_block, hidden_block, 1)
        weight_cols = lax.dynamic_slice_in_dim(weight, position * hidden_block, hidden_block, 1)
        product = lax.dot_general(grad_cols, weight_cols, (((1,), (1,)), ((), ())), preferred_element_type=jnp.float32).astype(jnp.bfloat16)
        product = lax.optimization_barrier(product).astype(jnp.float32)
        return (running + product, None)
    grad_sum, _ = lax.scan(bwd_term, jnp.zeros((TOKENS, D), jnp.float32), jnp.arange(N_DEP, dtype=jnp.int32))
    return (hidden, grad_sum.astype(jnp.bfloat16))
```

```python
import jax
import jax.numpy as jnp
from jax import lax
from jax.experimental import pallas as pl
from jax.experimental.pallas import tpu as pltpu
from jax.sharding import PartitionSpec as P

SHARES = (1, 1) + (2,) * 22 + (1, 1)
LAG = 2
DRAIN = 4
AHEAD, JOIN = 4, 2
OUTER, INNER = "outer", "inner"


def gelu_tanh(values):
    return jax.nn.gelu(values, approximate=True)


def wide(values):
    return values.astype(jnp.float32)


def narrow(values):
    return values.astype(jnp.bfloat16)


def plain_body(inputs, weight, grad_out):
    block_in = lax.all_gather(inputs, "dep", axis=0, tiled=True)
    full_weight = lax.all_gather(weight, "row", axis=0, tiled=True)
    partial_sum = jnp.dot(block_in, full_weight, preferred_element_type=jnp.float32)
    pre_act = wide(lax.psum_scatter(narrow(partial_sum), "col", scatter_dimension=0, tiled=True))
    activation, pullback = jax.vjp(gelu_tanh, pre_act)
    grad_local = narrow(pullback(wide(grad_out))[0])
    grad_block = lax.all_gather(grad_local, "col", axis=0, tiled=True)
    partial_grad = lax.dot_general(
        grad_block, full_weight, (((1,), (1,)), ((), ())), preferred_element_type=jnp.float32
    )
    grad_inputs = lax.psum_scatter(narrow(partial_grad), "dep", scatter_dimension=0, tiled=True)
    return (narrow(activation), grad_inputs)


class Tick:
    def __init__(self, rows):
        self.rows = rows
        self.operands, self.outputs, self.aliases, self.in_hbm = [], [], {}, []
        self.jobs = {"both": [], OUTER: [], INNER: []}

    def operand(self, array):
        for place, known in enumerate(self.operands):
            if known is array:
                return place
        self.operands.append(array)
        return len(self.operands) - 1

    def output(self, shape, alias=None):
        self.outputs.append(jax.ShapeDtypeStruct(shape, jnp.bfloat16))
        if alias is not None:
            self.aliases[self.operand(alias)] = len(self.outputs) - 1
        return len(self.outputs) - 1

    def source(self, where, height, width):
        array, row, column = where
        return (self.operand(array), row, column, height, width)

    def copy(self, role, where, to, height, width):
        self.jobs[role].append(("copy", [self.source(where, height, width)], [to]))

    def sum(self, role, wheres, to, width):
        self.jobs[role].append(("sum", [self.source(w, self.rows, width) for w in wheres], [to]))

    def gelu(self, role, wheres, out_where, hidden_to, grad_to, width):
        sources = [self.source(w, self.rows, width) for w in wheres + [out_where]]
        self.jobs[role].append(("gelu", sources, [hidden_to] + grad_to))

    def run(self, outer, token):
        rows = self.rows
        n_in, n_out = len(self.operands), len(self.outputs)
        computed = [job for jobs in self.jobs.values() for job in jobs if job[0] != "copy"]
        widest = max([job[1][0][4] for job in computed], default=128)
        slots = 1 + max(
            sum(len(job[1]) + 2 for job in jobs if job[0] != "copy") for jobs in self.jobs.values()
        )
        copies = 1 + sum(len(job[1]) + len(job[2]) for jobs in self.jobs.values() for job in jobs)

        def kernel(outer_ref, *refs):
            ins, outs = refs[1 : 1 + n_in], refs[1 + n_in : 1 + n_in + n_out]
            token_ref, buffer, sems = refs[1 + n_in + n_out :]
            token_ref[...] = jnp.zeros_like(token_ref)
            counter = [0]

            def begin(source, target):
                handle = pltpu.make_async_copy(source, target, sems.at[counter[0]])
                counter[0] += 1
                handle.start()
                return handle

            def window(ref, row, column, height, width):
                return ref.at[pl.ds(row, height), pl.ds(column, width)]

            def do(jobs):
                pending, loads, slot = [], [], 0
                for kind, sources, _ in jobs:
                    if kind != "copy":
                        handles, places = [], []
                        for place, row, column, height, width in sources:
                            spot = buffer.at[slot, :, pl.ds(0, width)]
                            handles.append(begin(window(ins[place], row, column, height, width), spot))
                            places.append(slot)
                            slot += 1
                        loads.append((handles, places))
                for kind, sources, targets in jobs:
                    if kind == "copy":
                        place, row, column, height, width = sources[0]
                        to, to_row, to_column = targets[0]
                        pending.append(
                            begin(
                                window(ins[place], row, column, height, width),
                                window(outs[to], to_row, to_column, height, width),
                            )
                        )
                for kind, sources, targets in jobs:
                    if kind == "copy":
                        continue
                    width = sources[0][4]
                    handles, places = loads.pop(0)
                    for handle in handles:
                        handle.wait()
                    terms = [wide(buffer[p, :, :width]) for p in places]
                    results = []
                    if kind == "sum":
                        results.append(narrow(sum(terms[1:], terms[0])))
                        owners = [0]
                    else:
                        pre_act = sum(terms[1:-1], terms[0])
                        activation, pullback = jax.vjp(gelu_tanh, pre_act)
                        results.append(narrow(activation))
                        results.append(narrow(pullback(terms[-1])[0]))
                        owners = [0] + [1] * (len(targets) - 1)
                    for result in results:
                        buffer[slot, :, :width] = result
                        slot += 1
                    first = slot - len(results)
                    for owner, (to, row, column) in zip(owners, targets):
                        pending.append(
                            begin(
                                buffer.at[first + owner, :, pl.ds(0, width)],
                                window(outs[to], row, column, rows, width),
                            )
                        )
                return pending

            both = do(self.jobs["both"])
            for role, wanted in ((OUTER, 1), (INNER, 0)):
                if self.jobs[role]:

                    @pl.when(outer_ref[0] == wanted)
                    def _():
                        for handle in do(self.jobs[role]):
                            handle.wait()

            for handle in both:
                handle.wait()

        operands = [
            pltpu.with_memory_space_constraint(array, pltpu.HBM) if any(array is known for known in self.in_hbm) else array
            for array in self.operands
        ]
        results = pl.pallas_call(
            kernel,
            out_shape=self.outputs + [jax.ShapeDtypeStruct((8, 128), jnp.float32)],
            in_specs=[pl.BlockSpec(memory_space=pltpu.SMEM)] + [pl.BlockSpec(memory_space=pl.ANY)] * (n_in + 1),
            out_specs=[pl.BlockSpec(memory_space=pl.ANY)] * n_out + [pl.BlockSpec(memory_space=pltpu.VMEM)],
            scratch_shapes=[
                pltpu.VMEM((slots, rows, widest), jnp.bfloat16),
                pltpu.SemaphoreType.DMA((copies,)),
            ],
            input_output_aliases={2 + place: to for place, to in self.aliases.items()},
            compiler_params=pltpu.CompilerParams(vmem_limit_bytes=12 * 2**20),
            cost_estimate=COST,
        )(outer, token, *operands)
        return results[:-1], results[-1]


COST = pl.CostEstimate(flops=10**10, bytes_accessed=1000, transcendentals=0)
COLUMNS = 256
VMEM = pl.BlockSpec(memory_space=pltpu.VMEM)


def forward(near_tokens, far_tokens, near, far):
    rows, width = near_tokens.shape[0], near.shape[1]

    def kernel(near_tokens_ref, far_tokens_ref, near_ref, far_ref, out_ref):
        @pl.loop(0, width // COLUMNS)
        def _(j):
            columns = pl.ds(pl.multiple_of(j * COLUMNS, COLUMNS), COLUMNS)
            part = jnp.dot(near_tokens_ref[...], near_ref[:, columns], preferred_element_type=jnp.float32)
            part = part + jnp.dot(far_tokens_ref[...], far_ref[:, columns], preferred_element_type=jnp.float32)
            out_ref[:, columns] = narrow(part)

    return pl.pallas_call(
        kernel,
        out_shape=jax.ShapeDtypeStruct((rows, width), jnp.bfloat16),
        in_specs=[VMEM] * 4,
        out_specs=VMEM,
        compiler_params=pltpu.CompilerParams(vmem_limit_bytes=12 * 2**20),
        cost_estimate=COST,
    )(near_tokens, far_tokens, near, far)


def backward(grad_block, near, far, total):
    rows = grad_block.shape[0]
    depth = near.shape[0]
    contract = (((1,), (1,)), ((), ()))

    def kernel(grad_ref, near_ref, far_ref, *refs):
        olds, news = refs[:-2], refs[-2:]

        @pl.loop(0, depth // COLUMNS)
        def _(j):
            columns = pl.ds(pl.multiple_of(j * COLUMNS, COLUMNS), COLUMNS)
            for place, part_ref in enumerate((near_ref, far_ref)):
                term = lax.dot_general(
                    grad_ref[...], part_ref[columns, :], contract, preferred_element_type=jnp.float32
                )
                news[place][:, columns] = olds[place][:, columns] + term if olds else term

    olds = list(total or [])
    return pl.pallas_call(
        kernel,
        out_shape=[jax.ShapeDtypeStruct((rows, depth), jnp.float32)] * 2,
        in_specs=[VMEM] * (3 + len(olds)),
        out_specs=[VMEM] * 2,
        input_output_aliases={3: 0, 4: 1} if olds else {},
        compiler_params=pltpu.CompilerParams(vmem_limit_bytes=12 * 2**20),
        cost_estimate=COST,
    )(grad_block, near, far, *olds)


def schedule(chunks):
    after = {"A": (None, 0), "B": ("A", LAG), "C": ("B", LAG), "G": ("C", LAG), "M": ("G", LAG), "T": ("G", LAG)}
    after.update({"U": ("M", LAG), "Z": ("U", LAG)})
    last = chunks + DRAIN
    when = {}
    for c in range(chunks):
        for item, (before, lag) in after.items():
            ready = None if before is None else when[c, before]
            when[c, item] = c if before is None else min(ready + lag, max(ready + 1, last))
    return when


def line_body(inputs, weight, grad_out):
    row, col, dep = (lax.axis_index(name) for name in ("row", "col", "dep"))
    mirrored = col >= 2
    outer = ((col == 0) | (col == 3)).astype(jnp.int32).reshape(1)
    swap_pairs = [(0, 1), (1, 0), (2, 3), (3, 2)]
    middle_pair = [(1, 2), (2, 1)]
    chip_pairs = [(0, 2), (2, 0), (1, 3), (3, 1)]
    core_pairs = [(0, 1), (1, 0), (2, 3), (3, 2)]

    depth, hidden_width = weight.shape
    rows = grad_out.shape[0]
    unit = hidden_width // sum(SHARES)
    sizes = [unit * share for share in SHARES]
    starts = [sum(sizes[:c]) for c in range(len(sizes))]
    chunks = len(sizes)
    when = schedule(chunks)
    last = max(when.values())

    def block(array, b):
        return array[b * rows : (b + 1) * rows]

    other_in = lax.ppermute(inputs, "dep", [(0, 1), (1, 0)])
    tokens = jnp.concatenate(
        [jnp.where(dep == 0, inputs, other_in), jnp.where(dep == 0, other_in, inputs)], axis=0
    )
    tokens = jnp.concatenate([jnp.where(mirrored, block(tokens, 3 - b), block(tokens, b)) for b in range(4)], axis=0)
    near_tokens, far_tokens = (
        jnp.concatenate([lax.dynamic_slice_in_dim(tokens, (row ^ flip) * depth, depth, 1) for flip in pair], axis=1)
        for pair in ((0, 2), (1, 3))
    )

    token = jnp.zeros((8, 128), jnp.float32)
    from_chip, near_weight, far_weight = {}, {}, {}
    place = {}
    hidden = total = None
    ask_at = {c: c - AHEAD for c in range(chunks)}
    join_at = {c: c - JOIN for c in range(chunks)}

    for tick in range(-AHEAD, last + 1):
        kernel = Tick(rows)
        kernel.in_hbm = [weight, grad_out]

        def now(item):
            return [c for c in range(chunks) if when[c, item] == tick]

        for c in now("A"):
            product = forward(near_tokens, far_tokens, near_weight[c], far_weight[c])
            for role in (OUTER, INNER):
                for b in range(4):
                    place[role, c, b] = (product, b * rows, 0)

        to_inner = [(c, "A%d" % b) for c in now("A") for b in (1, 2, 3)] + [(c, "first") for c in now("G")]
        to_outer = [(c, "C0") for c in now("C")]
        for item, name in (("G", "second"), ("T", "third"), ("U", "fourth")):
            to_outer += [(c, name) for c in now(item)]
        across = [(c, name) for c in now("B") for name in ("R1", "R0")]
        across += [(c, "third") for c in now("G")] + [(c, "fourth") for c in now("M")]

        def spots(message):
            found, column = {}, 0
            for c, name in message:
                found[c, name] = column
                column += sizes[c]
            return found, column

        inner_spots, inner_width = spots(to_inner)
        outer_spots, outer_width = spots(to_outer)
        across_spots, across_width = spots(across)
        swap_width = max(inner_width, outer_width)
        swap = kernel.output((rows, swap_width)) if swap_width else None
        middle = kernel.output((rows, across_width)) if across_width else None
        hidden_out = kernel.output(grad_out.shape, alias=hidden) if now("G") else None

        for c in now("A"):
            for b in (1, 2, 3):
                kernel.copy(OUTER, place[OUTER, c, b], (swap, 0, inner_spots[c, "A%d" % b]), rows, sizes[c])
        for c in now("B"):
            for b, name in ((2, "R1"), (3, "R0")):
                terms = [place[INNER, c, b], place[INNER, c, "A%d" % b]]
                kernel.sum(INNER, terms, (middle, 0, across_spots[c, name]), sizes[c])
        for c in now("C"):
            terms = [place[INNER, c, 0], place[INNER, c, "R0"]]
            kernel.sum(INNER, terms, (swap, 0, outer_spots[c, "C0"]), sizes[c])
        for c in now("G"):
            out_where, kept = (grad_out, 0, starts[c]), (hidden_out, 0, starts[c])
            terms = [place[OUTER, c, 0], place[OUTER, c, "C0"]]
            kernel.gelu(OUTER, terms, out_where, kept, [(swap, 0, inner_spots[c, "first"])], sizes[c])
            terms = [place[INNER, c, 1], place[INNER, c, "A1"], place[INNER, c, "R1"]]
            sent = [(swap, 0, outer_spots[c, "second"]), (middle, 0, across_spots[c, "third"])]
            kernel.gelu(INNER, terms, out_where, kept, sent, sizes[c])
        for c in now("M"):
            kernel.copy(INNER, place[INNER, c, "first"], (middle, 0, across_spots[c, "fourth"]), rows, sizes[c])
        for item, name in (("T", "third"), ("U", "fourth")):
            for c in now(item):
                kernel.copy(INNER, place[INNER, c, name], (swap, 0, outer_spots[c, name]), rows, sizes[c])
        blocks = {}
        for c in now("Z"):
            blocks[c] = kernel.output((4 * rows, sizes[c]))
            for role, names in ((OUTER, ("own", "second")), (INNER, ("first", "own"))):
                for b, name in enumerate(names + ("third", "fourth")):
                    kernel.copy(role, place[role, c, name], (blocks[c], b * rows, 0), rows, sizes[c])

        asked = {c: kernel.output((depth, sizes[c])) for c in range(chunks) if ask_at[c] == tick}
        for c, to in asked.items():
            kernel.copy("both", (weight, 0, starts[c]), (to, 0, 0), depth, sizes[c])
        joined = {c: kernel.output((2 * depth, sizes[c])) for c in range(chunks) if join_at[c] == tick}
        for c, to in joined.items():
            kernel.copy("both", (weight, 0, starts[c]), (to, 0, 0), depth, sizes[c])
            kernel.copy("both", (from_chip[c], 0, 0), (to, depth, 0), depth, sizes[c])
        for array in total or ():
            kernel.operand(array)
        if not kernel.outputs:
            continue

        outs, token = kernel.run(outer, token)

        if hidden_out is not None:
            hidden = outs[hidden_out]
        if swap is not None:
            arrived = lax.ppermute(outs[swap], "col", swap_pairs)
            for role, found in ((INNER, inner_spots), (OUTER, outer_spots)):
                for (c, name), column in found.items():
                    place[role, c, name] = (arrived, 0, column)
        if middle is not None:
            arrived = lax.ppermute(outs[middle], "col", middle_pair)
            for (c, name), column in across_spots.items():
                place[INNER, c, name] = (arrived, 0, column)
        for c in now("G"):
            place[OUTER, c, "own"] = (outs[swap], 0, inner_spots[c, "first"])
            place[INNER, c, "own"] = (outs[middle], 0, across_spots[c, "third"])
        for c, to in asked.items():
            from_chip[c] = lax.ppermute(outs[to], "row", chip_pairs)
        for c, to in joined.items():
            near_weight[c] = outs[to]
            far_weight[c] = lax.ppermute(outs[to], "row", core_pairs)
        for c in now("Z"):
            total = backward(outs[blocks[c]], near_weight.pop(c), far_weight.pop(c), total)

    half = 2 * rows
    other_half = jnp.where(mirrored, dep, 1 - dep) * half
    own_half = jnp.where(mirrored, 1 - dep, dep) * half
    result = []
    for part in total:
        sent = lax.ppermute(narrow(lax.dynamic_slice_in_dim(part, other_half, half, 0)), "dep", [(0, 1), (1, 0)])
        own = narrow(lax.dynamic_slice_in_dim(part, own_half, half, 0))
        result.append(narrow(wide(sent) + wide(own)))
    result = jnp.concatenate(result, axis=1)
    result = jnp.where(mirrored, jnp.concatenate([result[rows:], result[:rows]], axis=0), result)
    place_of = jnp.array([0, 2, 1, 3], jnp.int32)
    result = jnp.concatenate(
        [lax.dynamic_slice_in_dim(result, place_of[row ^ j] * depth, depth, 1) for j in range(4)], axis=1
    )
    return (hidden, result)


def solution(mesh):
    sizes = tuple(mesh.shape[name] for name in ("row", "col", "dep"))
    body = line_body if sizes == (4, 4, 2) else plain_body
    placed = (P(("row", "dep"), "col"), P(("col", "row"), "dep"), P(("row", "col"), "dep"))
    return jax.shard_map(
        body,
        mesh=mesh,
        in_specs=placed,
        out_specs=(P(("row", "col"), "dep"), P(("row", "dep"), "col")),
        check_vma=False,
    )
```

```python
import jax
import jax.numpy as jnp
from jax import lax
from jax.experimental import pallas as pl
from jax.experimental.pallas import tpu as pltpu
from jax.sharding import PartitionSpec as P

SHARES = ((1,), (1,)) + ((2,),) * 17 + ((1, 1),) * 6
LAG = 2
AHEAD, JOIN = 4, 2
OUTER, INNER = "outer", "inner"


def gelu_tanh(values):
    return jax.nn.gelu(values, approximate=True)


def wide(values):
    return values.astype(jnp.float32)


def narrow(values):
    return values.astype(jnp.bfloat16)


def plain_body(inputs, weight, grad_out):
    block_in = lax.all_gather(inputs, "dep", axis=0, tiled=True)
    full_weight = lax.all_gather(weight, "row", axis=0, tiled=True)
    partial_sum = jnp.dot(block_in, full_weight, preferred_element_type=jnp.float32)
    pre_act = wide(lax.psum_scatter(narrow(partial_sum), "col", scatter_dimension=0, tiled=True))
    activation, pullback = jax.vjp(gelu_tanh, pre_act)
    grad_local = narrow(pullback(wide(grad_out))[0])
    grad_block = lax.all_gather(grad_local, "col", axis=0, tiled=True)
    partial_grad = lax.dot_general(
        grad_block, full_weight, (((1,), (1,)), ((), ())), preferred_element_type=jnp.float32
    )
    grad_inputs = lax.psum_scatter(narrow(partial_grad), "dep", scatter_dimension=0, tiled=True)
    return (narrow(activation), grad_inputs)


VMEM = pl.BlockSpec(memory_space=pltpu.VMEM)


class Tick:
    def __init__(self, rows, far_arrays):
        self.rows, self.far_arrays = rows, far_arrays
        self.operands, self.outputs, self.idle = [], [], set()
        self.moves, self.shared = [], []
        self.jobs = {OUTER: [], INNER: []}

    def operand(self, array):
        for place, known in enumerate(self.operands):
            if known is array:
                return place
        self.operands.append(array)
        return len(self.operands) - 1

    def output(self, shape):
        self.outputs.append(jax.ShapeDtypeStruct(shape, jnp.bfloat16))
        return len(self.outputs) - 1

    def after(self, array):
        self.idle.add(self.operand(array))

    def source(self, where, height, width):
        array, row, column = where
        return (self.operand(array), pl.ds(row, height), pl.ds(column, width))

    def move(self, where, to, height, width):
        to, row, column = to
        self.moves.append((self.source(where, height, width), (to, pl.ds(row, height), pl.ds(column, width))))

    def sum(self, role, wheres, to, width):
        to, row, column = to
        target = (to, pl.ds(row, self.rows), pl.ds(column, width))
        self.jobs[role].append(("sum", [self.source(w, self.rows, width) for w in wheres], [target], None))

    def gelu(self, role, chunk, wheres, out_where, hidden_to, grad_to, width):
        known = [entry[0] for entry in self.shared]
        if chunk not in known:
            self.shared.append((chunk, self.source(out_where, self.rows, width), hidden_to, width))
            known.append(chunk)
        targets = [(to, pl.ds(row, self.rows), pl.ds(column, width)) for to, row, column in grad_to]
        sources = [self.source(w, self.rows, width) for w in wheres]
        self.jobs[role].append(("gelu", sources, targets, known.index(chunk)))

    def run(self, outer, token):
        rows, shared, moves = self.rows, self.shared, self.moves
        n_in, n_out = len(self.operands), len(self.outputs)
        slots = max(len(shared), 1)
        widest = max([entry[3] for entry in shared], default=128)

        def kernel(outer_ref, *refs):
            ins, outs = refs[1 : 1 + n_in], refs[1 + n_in : 1 + n_in + n_out]
            token_ref, loaded, sems = refs[1 + n_in + n_out :]
            token_ref[...] = jnp.zeros_like(token_ref)
            counter = [0]

            def begin(source, target):
                handle = pltpu.make_async_copy(source, target, sems.at[counter[0]])
                counter[0] += 1
                handle.start()
                return handle

            def window(buffers, spot):
                place, rows_at, columns_at = spot
                return buffers[place].at[rows_at, columns_at]

            def read(spot):
                place, rows_at, columns_at = spot
                return ins[place][rows_at, columns_at]

            def write(spot, value):
                place, rows_at, columns_at = spot
                outs[place][rows_at, columns_at] = value

            def by_role(wanted_kind, do):
                for role, wanted in ((OUTER, 1), (INNER, 0)):
                    jobs = [job for job in self.jobs[role] if job[0] == wanted_kind]
                    if jobs:

                        @pl.when(outer_ref[0] == wanted)
                        def _():
                            for job in jobs:
                                do(*job[1:])

            def do_sum(sources, targets, _):
                value = read(sources[0])
                if len(sources) > 1:
                    value = narrow(sum((wide(read(s)) for s in sources[1:]), wide(value)))
                write(targets[0], value)

            def do_gelu(sources, targets, slot):
                width = shared[slot][3]
                pre_act = sum((wide(read(s)) for s in sources[1:]), wide(read(sources[0])))
                activation, pullback = jax.vjp(gelu_tanh, pre_act)
                outs[shared[slot][2]][...] = narrow(activation)
                grad = narrow(pullback(wide(loaded[slot, :, :width]))[0])
                for target in targets:
                    write(target, grad)

            loads = [
                begin(window(ins, entry[1]), loaded.at[slot, :, pl.ds(0, entry[3])])
                for slot, entry in enumerate(shared)
            ]
            pending = [begin(window(ins, source), window(outs, target)) for source, target in moves]
            by_role("sum", do_sum)
            for handle in loads:
                handle.wait()
            by_role("gelu", do_gelu)
            for handle in pending:
                handle.wait()

        def is_far(array):
            return any(array is known for known in self.far_arrays)

        operands = [
            pltpu.with_memory_space_constraint(array, pltpu.HBM) if is_far(array) else array for array in self.operands
        ]
        anywhere = pl.BlockSpec(memory_space=pl.ANY)
        results = pl.pallas_call(
            kernel,
            out_shape=self.outputs + [jax.ShapeDtypeStruct((8, 128), jnp.float32)],
            in_specs=[pl.BlockSpec(memory_space=pltpu.SMEM), anywhere]
            + [anywhere if is_far(x) or place in self.idle else VMEM for place, x in enumerate(self.operands)],
            out_specs=[VMEM] * (n_out + 1),
            scratch_shapes=[
                pltpu.VMEM((slots, rows, widest), jnp.bfloat16),
                pltpu.SemaphoreType.DMA((slots + len(moves),)),
            ],
            compiler_params=pltpu.CompilerParams(vmem_limit_bytes=12 * 2**20),
            cost_estimate=COST,
        )(outer, token, *operands)
        return results[:-1], results[-1]


COST = pl.CostEstimate(flops=10**10, bytes_accessed=1000, transcendentals=0)
COLUMNS = 256


def forward(near_tokens, far_tokens, near, far):
    rows, width = near_tokens.shape[0], near.shape[1]

    def kernel(near_tokens_ref, far_tokens_ref, near_ref, far_ref, out_ref):
        @pl.loop(0, width // COLUMNS)
        def _(j):
            columns = pl.ds(pl.multiple_of(j * COLUMNS, COLUMNS), COLUMNS)
            part = jnp.dot(near_tokens_ref[...], near_ref[:, columns], preferred_element_type=jnp.float32)
            part = part + jnp.dot(far_tokens_ref[...], far_ref[:, columns], preferred_element_type=jnp.float32)
            out_ref[:, columns] = narrow(part)

    return pl.pallas_call(
        kernel,
        out_shape=jax.ShapeDtypeStruct((rows, width), jnp.bfloat16),
        in_specs=[VMEM] * 4,
        out_specs=VMEM,
        compiler_params=pltpu.CompilerParams(vmem_limit_bytes=12 * 2**20),
        cost_estimate=COST,
    )(near_tokens, far_tokens, near, far)


def backward(grad_block, near, far, total):
    rows = grad_block.shape[0]
    depth = near.shape[0]
    contract = (((1,), (1,)), ((), ()))

    def kernel(grad_ref, near_ref, far_ref, *refs):
        olds, news = refs[:-2], refs[-2:]

        @pl.loop(0, depth // COLUMNS)
        def _(j):
            columns = pl.ds(pl.multiple_of(j * COLUMNS, COLUMNS), COLUMNS)
            for place, part_ref in enumerate((near_ref, far_ref)):
                term = lax.dot_general(
                    grad_ref[...], part_ref[columns, :], contract, preferred_element_type=jnp.float32
                )
                news[place][:, columns] = olds[place][:, columns] + term if olds else term

    olds = list(total or [])
    return pl.pallas_call(
        kernel,
        out_shape=[jax.ShapeDtypeStruct((rows, depth), jnp.float32)] * 2,
        in_specs=[VMEM] * (3 + len(olds)),
        out_specs=[VMEM] * 2,
        input_output_aliases={3: 0, 4: 1} if olds else {},
        compiler_params=pltpu.CompilerParams(vmem_limit_bytes=12 * 2**20),
        cost_estimate=COST,
    )(grad_block, near, far, *olds)


def schedule(groups):
    after = {"A": (None, 0), "B": ("A", LAG), "C": ("B", LAG), "G": ("C", LAG), "M": ("G", LAG), "T": ("G", LAG)}
    after.update({"U": ("M", LAG), "Z": ("U", LAG)})
    chunks = sum(len(group) for group in groups)
    when = {}
    for c in range(chunks):
        for item, (before, lag) in after.items():
            when[c, item] = c if before is None else when[c, before] + lag
    for group in groups:
        for c in group:
            when[c, "Z"] = when[group[-1], "Z"]
    return when


def line_body(inputs, weight, grad_out):
    row, col, dep = (lax.axis_index(name) for name in ("row", "col", "dep"))
    mirrored = col >= 2
    outer = ((col == 0) | (col == 3)).astype(jnp.int32).reshape(1)
    swap_pairs = [(0, 1), (1, 0), (2, 3), (3, 2)]
    middle_pair = [(1, 2), (2, 1)]
    chip_pairs = [(0, 2), (2, 0), (1, 3), (3, 1)]
    core_pairs = [(0, 1), (1, 0), (2, 3), (3, 2)]

    depth, hidden_width = weight.shape
    rows = grad_out.shape[0]
    shares = [share for group in SHARES for share in group]
    unit = hidden_width // sum(shares)
    sizes = [unit * share for share in shares]
    starts = [sum(sizes[:c]) for c in range(len(sizes))]
    chunks = len(sizes)
    groups = []
    for group in SHARES:
        first = groups[-1][-1] + 1 if groups else 0
        groups.append(list(range(first, first + len(group))))
    widths = [sum(sizes[c] for c in group) for group in groups]
    when = schedule(groups)
    last = max(when.values())

    def block(array, b):
        return array[b * rows : (b + 1) * rows]

    other_in = lax.ppermute(inputs, "dep", [(0, 1), (1, 0)])
    tokens = jnp.concatenate(
        [jnp.where(dep == 0, inputs, other_in), jnp.where(dep == 0, other_in, inputs)], axis=0
    )
    tokens = jnp.concatenate([jnp.where(mirrored, block(tokens, 3 - b), block(tokens, b)) for b in range(4)], axis=0)
    near_tokens, far_tokens = (
        jnp.concatenate([lax.dynamic_slice_in_dim(tokens, (row ^ flip) * depth, depth, 1) for flip in pair], axis=1)
        for pair in ((0, 2), (1, 3))
    )

    token = jnp.zeros((8, 128), jnp.float32)
    from_chip, near_weight, far_weight = {}, {}, {}
    place = {}
    hidden, total = {}, None

    for tick in range(-AHEAD, last + 1):
        kernel = Tick(rows, [weight, grad_out])

        def now(item):
            return [c for c in range(chunks) if when[c, item] == tick]

        def starting(ahead):
            return [g for g, group in enumerate(groups) if group[0] - ahead == tick]

        for g in starting(0):
            product = forward(near_tokens, far_tokens, near_weight[g], far_weight[g])
            for c in groups[g]:
                for role in (OUTER, INNER):
                    for b in range(4):
                        place[role, c, b] = (product, b * rows, starts[c] - starts[groups[g][0]])

        to_inner = [(c, "A%d" % b) for c in now("A") for b in (1, 2, 3)] + [(c, "first") for c in now("G")]
        to_outer = [(c, "C0") for c in now("C")]
        for item, name in (("G", "second"), ("T", "third"), ("U", "fourth")):
            to_outer += [(c, name) for c in now(item)]
        across = [(c, name) for c in now("B") for name in ("R1", "R0")]
        across += [(c, "third") for c in now("G")] + [(c, "fourth") for c in now("M")]

        def spots(message):
            found, column = {}, 0
            for c, name in message:
                found[c, name] = column
                column += sizes[c]
            return found, column

        inner_spots, inner_width = spots(to_inner)
        outer_spots, outer_width = spots(to_outer)
        across_spots, across_width = spots(across)
        swap_width = max(inner_width, outer_width)
        swap = kernel.output((rows, swap_width)) if swap_width else None
        middle = kernel.output((rows, across_width)) if across_width else None
        hidden_out = {c: kernel.output((rows, sizes[c])) for c in now("G")}

        for c in now("A"):
            for b in (1, 2, 3):
                kernel.sum(OUTER, [place[OUTER, c, b]], (swap, 0, inner_spots[c, "A%d" % b]), sizes[c])
        for c in now("B"):
            for b, name in ((2, "R1"), (3, "R0")):
                terms = [place[INNER, c, b], place[INNER, c, "A%d" % b]]
                kernel.sum(INNER, terms, (middle, 0, across_spots[c, name]), sizes[c])
        for c in now("C"):
            terms = [place[INNER, c, 0], place[INNER, c, "R0"]]
            kernel.sum(INNER, terms, (swap, 0, outer_spots[c, "C0"]), sizes[c])
        for c in now("G"):
            out_where, kept = (grad_out, 0, starts[c]), hidden_out[c]
            terms = [place[OUTER, c, 0], place[OUTER, c, "C0"]]
            kernel.gelu(OUTER, c, terms, out_where, kept, [(swap, 0, inner_spots[c, "first"])], sizes[c])
            terms = [place[INNER, c, 1], place[INNER, c, "A1"], place[INNER, c, "R1"]]
            sent = [(swap, 0, outer_spots[c, "second"]), (middle, 0, across_spots[c, "third"])]
            kernel.gelu(INNER, c, terms, out_where, kept, sent, sizes[c])
        for c in now("M"):
            kernel.sum(INNER, [place[INNER, c, "first"]], (middle, 0, across_spots[c, "fourth"]), sizes[c])
        for item, name in (("T", "third"), ("U", "fourth")):
            for c in now(item):
                kernel.sum(INNER, [place[INNER, c, name]], (swap, 0, outer_spots[c, name]), sizes[c])
        blocks = {}
        for g, group in enumerate(groups):
            if when[group[0], "Z"] != tick:
                continue
            blocks[g] = kernel.output((4 * rows, widths[g]))
            for c in group:
                column = starts[c] - starts[group[0]]
                for role, names in ((OUTER, ("own", "second")), (INNER, ("first", "own"))):
                    for b, name in enumerate(names + ("third", "fourth")):
                        kernel.sum(role, [place[role, c, name]], (blocks[g], b * rows, column), sizes[c])

        asked = {g: kernel.output((depth, widths[g])) for g in starting(AHEAD)}
        for g, to in asked.items():
            kernel.move((weight, 0, starts[groups[g][0]]), (to, 0, 0), depth, widths[g])
        joined = {g: kernel.output((2 * depth, widths[g])) for g in starting(JOIN)}
        for g, to in joined.items():
            kernel.move((weight, 0, starts[groups[g][0]]), (to, 0, 0), depth, widths[g])
            kernel.move((from_chip[g], 0, 0), (to, depth, 0), depth, widths[g])
        for array in total or ():
            kernel.after(array)
        if not kernel.outputs:
            continue

        outs, token = kernel.run(outer, token)

        for c, to in hidden_out.items():
            hidden[c] = outs[to]
        if swap is not None:
            arrived = lax.ppermute(outs[swap], "col", swap_pairs)
            for role, found in ((INNER, inner_spots), (OUTER, outer_spots)):
                for (c, name), column in found.items():
                    place[role, c, name] = (arrived, 0, column)
        if middle is not None:
            arrived = lax.ppermute(outs[middle], "col", middle_pair)
            for (c, name), column in across_spots.items():
                place[INNER, c, name] = (arrived, 0, column)
        for c in now("G"):
            place[OUTER, c, "own"] = (outs[swap], 0, inner_spots[c, "first"])
            place[INNER, c, "own"] = (outs[middle], 0, across_spots[c, "third"])
        for g, to in asked.items():
            from_chip[g] = lax.ppermute(outs[to], "row", chip_pairs)
        for g, to in joined.items():
            near_weight[g] = outs[to]
            far_weight[g] = lax.ppermute(outs[to], "row", core_pairs)
        for g, to in blocks.items():
            total = backward(outs[to], near_weight.pop(g), far_weight.pop(g), total)

    half = 2 * rows
    other_half = jnp.where(mirrored, dep, 1 - dep) * half
    own_half = jnp.where(mirrored, 1 - dep, dep) * half
    result = []
    for part in total:
        sent = lax.ppermute(narrow(lax.dynamic_slice_in_dim(part, other_half, half, 0)), "dep", [(0, 1), (1, 0)])
        own = narrow(lax.dynamic_slice_in_dim(part, own_half, half, 0))
        result.append(narrow(wide(sent) + wide(own)))
    result = jnp.concatenate(result, axis=1)
    result = jnp.where(mirrored, jnp.concatenate([result[rows:], result[:rows]], axis=0), result)
    place_of = jnp.array([0, 2, 1, 3], jnp.int32)
    result = jnp.concatenate(
        [lax.dynamic_slice_in_dim(result, place_of[row ^ j] * depth, depth, 1) for j in range(4)], axis=1
    )
    return (jnp.concatenate([hidden[c] for c in range(chunks)], axis=1), result)


def solution(mesh):
    sizes = tuple(mesh.shape[name] for name in ("row", "col", "dep"))
    body = line_body if sizes == (4, 4, 2) else plain_body
    placed = (P(("row", "dep"), "col"), P(("col", "row"), "dep"), P(("row", "col"), "dep"))
    return jax.shard_map(
        body,
        mesh=mesh,
        in_specs=placed,
        out_specs=(P(("row", "col"), "dep"), P(("row", "dep"), "col")),
        check_vma=False,
    )
```

```python
import jax
import jax.numpy as jnp
from jax import lax
from jax.experimental import pallas as pl
from jax.experimental.pallas import tpu as pltpu
from jax.sharding import PartitionSpec as P

SHARES = ((2,), (2,)) + ((3,),) * 30 + ((2,),)
LAG = 2
AHEAD, JOIN = 4, 2
OUTER, INNER = "outer", "inner"


def gelu_tanh(values):
    return jax.nn.gelu(values, approximate=True)


def wide(values):
    return values.astype(jnp.float32)


def narrow(values):
    return values.astype(jnp.bfloat16)


def plain_body(inputs, weight, grad_out):
    block_in = lax.all_gather(inputs, "dep", axis=0, tiled=True)
    full_weight = lax.all_gather(weight, "row", axis=0, tiled=True)
    partial_sum = jnp.dot(block_in, full_weight, preferred_element_type=jnp.float32)
    pre_act = wide(lax.psum_scatter(narrow(partial_sum), "col", scatter_dimension=0, tiled=True))
    activation, pullback = jax.vjp(gelu_tanh, pre_act)
    grad_local = narrow(pullback(wide(grad_out))[0])
    grad_block = lax.all_gather(grad_local, "col", axis=0, tiled=True)
    partial_grad = lax.dot_general(
        grad_block, full_weight, (((1,), (1,)), ((), ())), preferred_element_type=jnp.float32
    )
    grad_inputs = lax.psum_scatter(narrow(partial_grad), "dep", scatter_dimension=0, tiled=True)
    return (narrow(activation), grad_inputs)


VMEM = pl.BlockSpec(memory_space=pltpu.VMEM)


class Tick:
    def __init__(self, rows, far_arrays):
        self.rows, self.far_arrays = rows, far_arrays
        self.operands, self.outputs, self.idle = [], [], set()
        self.moves, self.shared = [], []
        self.jobs = {OUTER: [], INNER: []}

    def operand(self, array):
        for place, known in enumerate(self.operands):
            if known is array:
                return place
        self.operands.append(array)
        return len(self.operands) - 1

    def output(self, shape):
        self.outputs.append(jax.ShapeDtypeStruct(shape, jnp.bfloat16))
        return len(self.outputs) - 1

    def after(self, array):
        self.idle.add(self.operand(array))

    def source(self, where, height, width):
        array, row, column = where
        return (self.operand(array), pl.ds(row, height), pl.ds(column, width))

    def move(self, where, to, height, width):
        to, row, column = to
        self.moves.append((self.source(where, height, width), (to, pl.ds(row, height), pl.ds(column, width))))

    def sum(self, role, wheres, to, width):
        to, row, column = to
        target = (to, pl.ds(row, self.rows), pl.ds(column, width))
        self.jobs[role].append(("sum", [self.source(w, self.rows, width) for w in wheres], [target], None))

    def gelu(self, role, chunk, wheres, out_where, hidden_to, grad_to, width):
        known = [entry[0] for entry in self.shared]
        if chunk not in known:
            self.shared.append((chunk, self.source(out_where, self.rows, width), hidden_to, width))
            known.append(chunk)
        targets = [(to, pl.ds(row, self.rows), pl.ds(column, width)) for to, row, column in grad_to]
        sources = [self.source(w, self.rows, width) for w in wheres]
        self.jobs[role].append(("gelu", sources, targets, known.index(chunk)))

    def run(self, outer, token):
        rows, shared, moves = self.rows, self.shared, self.moves
        n_in, n_out = len(self.operands), len(self.outputs)
        slots = max(len(shared), 1)
        widest = max([entry[3] for entry in shared], default=128)

        def kernel(outer_ref, *refs):
            ins, outs = refs[1 : 1 + n_in], refs[1 + n_in : 1 + n_in + n_out]
            token_ref, loaded, sems = refs[1 + n_in + n_out :]
            token_ref[...] = jnp.zeros_like(token_ref)
            counter = [0]

            def begin(source, target):
                handle = pltpu.make_async_copy(source, target, sems.at[counter[0]])
                counter[0] += 1
                handle.start()
                return handle

            def window(buffers, spot):
                place, rows_at, columns_at = spot
                return buffers[place].at[rows_at, columns_at]

            def read(spot):
                place, rows_at, columns_at = spot
                return ins[place][rows_at, columns_at]

            def write(spot, value):
                place, rows_at, columns_at = spot
                outs[place][rows_at, columns_at] = value

            def by_role(wanted_kind, do):
                for role, wanted in ((OUTER, 1), (INNER, 0)):
                    jobs = [job for job in self.jobs[role] if job[0] == wanted_kind]
                    if jobs:

                        @pl.when(outer_ref[0] == wanted)
                        def _():
                            for job in jobs:
                                do(*job[1:])

            def do_sum(sources, targets, _):
                value = read(sources[0])
                if len(sources) > 1:
                    value = narrow(sum((wide(read(s)) for s in sources[1:]), wide(value)))
                write(targets[0], value)

            def do_gelu(sources, targets, slot):
                width = shared[slot][3]
                pre_act = sum((wide(read(s)) for s in sources[1:]), wide(read(sources[0])))
                activation, pullback = jax.vjp(gelu_tanh, pre_act)
                outs[shared[slot][2]][...] = narrow(activation)
                grad = narrow(pullback(wide(loaded[slot, :, :width]))[0])
                for target in targets:
                    write(target, grad)

            loads = [
                begin(window(ins, entry[1]), loaded.at[slot, :, pl.ds(0, entry[3])])
                for slot, entry in enumerate(shared)
            ]
            pending = [begin(window(ins, source), window(outs, target)) for source, target in moves]
            by_role("sum", do_sum)
            for handle in loads:
                handle.wait()
            by_role("gelu", do_gelu)
            for handle in pending:
                handle.wait()

        def is_far(array):
            return any(array is known for known in self.far_arrays)

        operands = [
            pltpu.with_memory_space_constraint(array, pltpu.HBM) if is_far(array) else array for array in self.operands
        ]
        anywhere = pl.BlockSpec(memory_space=pl.ANY)
        results = pl.pallas_call(
            kernel,
            out_shape=self.outputs + [jax.ShapeDtypeStruct((8, 128), jnp.float32)],
            in_specs=[pl.BlockSpec(memory_space=pltpu.SMEM), anywhere]
            + [anywhere if is_far(x) or place in self.idle else VMEM for place, x in enumerate(self.operands)],
            out_specs=[VMEM] * (n_out + 1),
            scratch_shapes=[
                pltpu.VMEM((slots, rows, widest), jnp.bfloat16),
                pltpu.SemaphoreType.DMA((slots + len(moves),)),
            ],
            compiler_params=pltpu.CompilerParams(vmem_limit_bytes=12 * 2**20),
            cost_estimate=COST,
        )(outer, token, *operands)
        return results[:-1], results[-1]


COST = pl.CostEstimate(flops=10**10, bytes_accessed=1000, transcendentals=0)
COLUMNS = 256


def forward(near_tokens, far_tokens, near, far):
    rows, width = near_tokens.shape[0], near.shape[1]

    def kernel(near_tokens_ref, far_tokens_ref, near_ref, far_ref, out_ref):
        tile = COLUMNS if width % COLUMNS == 0 else width

        @pl.loop(0, width // tile)
        def _(j):
            columns = pl.ds(pl.multiple_of(j * tile, tile), tile)
            part = jnp.dot(near_tokens_ref[...], near_ref[:, columns], preferred_element_type=jnp.float32)
            part = part + jnp.dot(far_tokens_ref[...], far_ref[:, columns], preferred_element_type=jnp.float32)
            out_ref[:, columns] = narrow(part)

    return pl.pallas_call(
        kernel,
        out_shape=jax.ShapeDtypeStruct((rows, width), jnp.bfloat16),
        in_specs=[VMEM] * 4,
        out_specs=VMEM,
        compiler_params=pltpu.CompilerParams(vmem_limit_bytes=12 * 2**20),
        cost_estimate=COST,
    )(near_tokens, far_tokens, near, far)


def backward(grad_block, near, far, total):
    rows = grad_block.shape[0]
    depth = near.shape[0]
    contract = (((1,), (1,)), ((), ()))

    def kernel(grad_ref, near_ref, far_ref, *refs):
        olds, news = refs[:-2], refs[-2:]

        @pl.loop(0, depth // COLUMNS)
        def _(j):
            columns = pl.ds(pl.multiple_of(j * COLUMNS, COLUMNS), COLUMNS)
            for place, part_ref in enumerate((near_ref, far_ref)):
                term = lax.dot_general(
                    grad_ref[...], part_ref[columns, :], contract, preferred_element_type=jnp.float32
                )
                news[place][:, columns] = olds[place][:, columns] + term if olds else term

    olds = list(total or [])
    return pl.pallas_call(
        kernel,
        out_shape=[jax.ShapeDtypeStruct((rows, depth), jnp.float32)] * 2,
        in_specs=[VMEM] * (3 + len(olds)),
        out_specs=[VMEM] * 2,
        input_output_aliases={3: 0, 4: 1} if olds else {},
        compiler_params=pltpu.CompilerParams(vmem_limit_bytes=12 * 2**20),
        cost_estimate=COST,
    )(grad_block, near, far, *olds)


def schedule(groups):
    after = {"A": (None, 0), "B": ("A", LAG), "C": ("B", LAG), "G": ("C", LAG), "M": ("G", LAG), "T": ("G", LAG)}
    after.update({"U": ("M", LAG), "Z": ("U", LAG)})
    chunks = sum(len(group) for group in groups)
    when = {}
    for c in range(chunks):
        for item, (before, lag) in after.items():
            when[c, item] = c if before is None else when[c, before] + lag
    for group in groups:
        joined = when[group[-1], "Z"] + (len(group) > 1 and group is not groups[-1])
        for c in group:
            when[c, "Z"] = joined
    return when


def line_body(inputs, weight, grad_out):
    row, col, dep = (lax.axis_index(name) for name in ("row", "col", "dep"))
    mirrored = col >= 2
    outer = ((col == 0) | (col == 3)).astype(jnp.int32).reshape(1)
    swap_pairs = [(0, 1), (1, 0), (2, 3), (3, 2)]
    middle_pair = [(1, 2), (2, 1)]
    chip_pairs = [(0, 2), (2, 0), (1, 3), (3, 1)]
    core_pairs = [(0, 1), (1, 0), (2, 3), (3, 2)]

    depth, hidden_width = weight.shape
    rows = grad_out.shape[0]
    shares = [share for group in SHARES for share in group]
    unit = hidden_width // sum(shares)
    sizes = [unit * share for share in shares]
    starts = [sum(sizes[:c]) for c in range(len(sizes))]
    chunks = len(sizes)
    groups = []
    for group in SHARES:
        first = groups[-1][-1] + 1 if groups else 0
        groups.append(list(range(first, first + len(group))))
    widths = [sum(sizes[c] for c in group) for group in groups]
    when = schedule(groups)
    last = max(when.values())

    def block(array, b):
        return array[b * rows : (b + 1) * rows]

    other_in = lax.ppermute(inputs, "dep", [(0, 1), (1, 0)])
    tokens = jnp.concatenate(
        [jnp.where(dep == 0, inputs, other_in), jnp.where(dep == 0, other_in, inputs)], axis=0
    )
    tokens = jnp.concatenate([jnp.where(mirrored, block(tokens, 3 - b), block(tokens, b)) for b in range(4)], axis=0)
    near_tokens, far_tokens = (
        jnp.concatenate([lax.dynamic_slice_in_dim(tokens, (row ^ flip) * depth, depth, 1) for flip in pair], axis=1)
        for pair in ((0, 2), (1, 3))
    )

    token = jnp.zeros((8, 128), jnp.float32)
    from_chip, near_weight, far_weight = {}, {}, {}
    place = {}
    hidden, total = {}, None

    for tick in range(-AHEAD, last + 1):
        kernel = Tick(rows, [weight, grad_out])

        def now(item):
            return [c for c in range(chunks) if when[c, item] == tick]

        def starting(ahead):
            return [g for g, group in enumerate(groups) if group[0] - ahead == tick]

        for g in starting(0):
            product = forward(near_tokens, far_tokens, near_weight[g], far_weight[g])
            for c in groups[g]:
                for role in (OUTER, INNER):
                    for b in range(4):
                        place[role, c, b] = (product, b * rows, starts[c] - starts[groups[g][0]])

        to_inner = [(c, "A%d" % b) for c in now("A") for b in (1, 2, 3)] + [(c, "first") for c in now("G")]
        to_outer = [(c, "C0") for c in now("C")]
        for item, name in (("G", "second"), ("T", "third"), ("U", "fourth")):
            to_outer += [(c, name) for c in now(item)]
        across = [(c, name) for c in now("B") for name in ("R1", "R0")]
        across += [(c, "third") for c in now("G")] + [(c, "fourth") for c in now("M")]

        def spots(message):
            found, column = {}, 0
            for c, name in message:
                found[c, name] = column
                column += sizes[c]
            return found, column

        inner_spots, inner_width = spots(to_inner)
        outer_spots, outer_width = spots(to_outer)
        across_spots, across_width = spots(across)
        swap_width = max(inner_width, outer_width)
        swap = kernel.output((rows, swap_width)) if swap_width else None
        middle = kernel.output((rows, across_width)) if across_width else None
        hidden_out = {c: kernel.output((rows, sizes[c])) for c in now("G")}

        for c in now("A"):
            for b in (1, 2, 3):
                kernel.sum(OUTER, [place[OUTER, c, b]], (swap, 0, inner_spots[c, "A%d" % b]), sizes[c])
        for c in now("B"):
            for b, name in ((2, "R1"), (3, "R0")):
                terms = [place[INNER, c, b], place[INNER, c, "A%d" % b]]
                kernel.sum(INNER, terms, (middle, 0, across_spots[c, name]), sizes[c])
        for c in now("C"):
            terms = [place[INNER, c, 0], place[INNER, c, "R0"]]
            kernel.sum(INNER, terms, (swap, 0, outer_spots[c, "C0"]), sizes[c])
        for c in now("G"):
            out_where, kept = (grad_out, 0, starts[c]), hidden_out[c]
            terms = [place[OUTER, c, 0], place[OUTER, c, "C0"]]
            kernel.gelu(OUTER, c, terms, out_where, kept, [(swap, 0, inner_spots[c, "first"])], sizes[c])
            terms = [place[INNER, c, 1], place[INNER, c, "A1"], place[INNER, c, "R1"]]
            sent = [(swap, 0, outer_spots[c, "second"]), (middle, 0, across_spots[c, "third"])]
            kernel.gelu(INNER, c, terms, out_where, kept, sent, sizes[c])
        for c in now("M"):
            kernel.sum(INNER, [place[INNER, c, "first"]], (middle, 0, across_spots[c, "fourth"]), sizes[c])
        for item, name in (("T", "third"), ("U", "fourth")):
            for c in now(item):
                kernel.sum(INNER, [place[INNER, c, name]], (swap, 0, outer_spots[c, name]), sizes[c])
        blocks = {}
        for g, group in enumerate(groups):
            if when[group[0], "Z"] != tick:
                continue
            blocks[g] = kernel.output((4 * rows, widths[g]))
            for c in group:
                column = starts[c] - starts[group[0]]
                for role, names in ((OUTER, ("own", "second")), (INNER, ("first", "own"))):
                    for b, name in enumerate(names + ("third", "fourth")):
                        kernel.sum(role, [place[role, c, name]], (blocks[g], b * rows, column), sizes[c])

        asked = {g: kernel.output((depth, widths[g])) for g in starting(AHEAD)}
        for g, to in asked.items():
            kernel.move((weight, 0, starts[groups[g][0]]), (to, 0, 0), depth, widths[g])
        joined = {g: kernel.output((2 * depth, widths[g])) for g in starting(JOIN)}
        for g, to in joined.items():
            kernel.move((weight, 0, starts[groups[g][0]]), (to, 0, 0), depth, widths[g])
            kernel.move((from_chip[g], 0, 0), (to, depth, 0), depth, widths[g])
        for array in total or ():
            kernel.after(array)
        if not kernel.outputs:
            continue

        outs, token = kernel.run(outer, token)

        for c, to in hidden_out.items():
            hidden[c] = outs[to]
        if swap is not None:
            arrived = lax.ppermute(outs[swap], "col", swap_pairs)
            for role, found in ((INNER, inner_spots), (OUTER, outer_spots)):
                for (c, name), column in found.items():
                    place[role, c, name] = (arrived, 0, column)
        if middle is not None:
            arrived = lax.ppermute(outs[middle], "col", middle_pair)
            for (c, name), column in across_spots.items():
                place[INNER, c, name] = (arrived, 0, column)
        for c in now("G"):
            place[OUTER, c, "own"] = (outs[swap], 0, inner_spots[c, "first"])
            place[INNER, c, "own"] = (outs[middle], 0, across_spots[c, "third"])
        for g, to in asked.items():
            from_chip[g] = lax.ppermute(outs[to], "row", chip_pairs)
        for g, to in joined.items():
            near_weight[g] = outs[to]
            far_weight[g] = lax.ppermute(outs[to], "row", core_pairs)
        for g, to in blocks.items():
            total = backward(outs[to], near_weight.pop(g), far_weight.pop(g), total)

    half = 2 * rows
    other_half = jnp.where(mirrored, dep, 1 - dep) * half
    own_half = jnp.where(mirrored, 1 - dep, dep) * half
    result = []
    for part in total:
        sent = lax.ppermute(narrow(lax.dynamic_slice_in_dim(part, other_half, half, 0)), "dep", [(0, 1), (1, 0)])
        own = narrow(lax.dynamic_slice_in_dim(part, own_half, half, 0))
        result.append(narrow(wide(sent) + wide(own)))
    result = jnp.concatenate(result, axis=1)
    result = jnp.where(mirrored, jnp.concatenate([result[rows:], result[:rows]], axis=0), result)
    place_of = jnp.array([0, 2, 1, 3], jnp.int32)
    result = jnp.concatenate(
        [lax.dynamic_slice_in_dim(result, place_of[row ^ j] * depth, depth, 1) for j in range(4)], axis=1
    )
    return (jnp.concatenate([hidden[c] for c in range(chunks)], axis=1), result)


def solution(mesh):
    sizes = tuple(mesh.shape[name] for name in ("row", "col", "dep"))
    body = line_body if sizes == (4, 4, 2) else plain_body
    placed = (P(("row", "dep"), "col"), P(("col", "row"), "dep"), P(("row", "col"), "dep"))
    return jax.shard_map(
        body,
        mesh=mesh,
        in_specs=placed,
        out_specs=(P(("row", "col"), "dep"), P(("row", "dep"), "col")),
        check_vma=False,
    )
```

```python
import jax
import jax.numpy as jnp
from jax import lax
from jax.experimental import pallas as pl
from jax.experimental.pallas import tpu as pltpu
from jax.sharding import PartitionSpec as P

SHARES = ((1,), (1,)) + ((2,),) * 19 + ((1, 1),) * 4
LAG = 2
AHEAD, JOIN = 4, 2
OUTER, INNER = "outer", "inner"


def gelu_tanh(values):
    return jax.nn.gelu(values, approximate=True)


def wide(values):
    return values.astype(jnp.float32)


def narrow(values):
    return values.astype(jnp.bfloat16)


def plain_body(inputs, weight, grad_out):
    block_in = lax.all_gather(inputs, "dep", axis=0, tiled=True)
    full_weight = lax.all_gather(weight, "row", axis=0, tiled=True)
    partial_sum = jnp.dot(block_in, full_weight, preferred_element_type=jnp.float32)
    pre_act = wide(lax.psum_scatter(narrow(partial_sum), "col", scatter_dimension=0, tiled=True))
    activation, pullback = jax.vjp(gelu_tanh, pre_act)
    grad_local = narrow(pullback(wide(grad_out))[0])
    grad_block = lax.all_gather(grad_local, "col", axis=0, tiled=True)
    partial_grad = lax.dot_general(
        grad_block, full_weight, (((1,), (1,)), ((), ())), preferred_element_type=jnp.float32
    )
    grad_inputs = lax.psum_scatter(narrow(partial_grad), "dep", scatter_dimension=0, tiled=True)
    return (narrow(activation), grad_inputs)


VMEM = pl.BlockSpec(memory_space=pltpu.VMEM)


class Tick:
    def __init__(self, rows, far_arrays):
        self.rows, self.far_arrays = rows, far_arrays
        self.operands, self.outputs, self.idle = [], [], set()
        self.moves, self.shared = [], []
        self.jobs = {OUTER: [], INNER: []}

    def operand(self, array):
        for place, known in enumerate(self.operands):
            if known is array:
                return place
        self.operands.append(array)
        return len(self.operands) - 1

    def output(self, shape):
        self.outputs.append(jax.ShapeDtypeStruct(shape, jnp.bfloat16))
        return len(self.outputs) - 1

    def after(self, array):
        self.idle.add(self.operand(array))

    def source(self, where, height, width):
        array, row, column = where
        return (self.operand(array), pl.ds(row, height), pl.ds(column, width))

    def move(self, where, to, height, width):
        to, row, column = to
        self.moves.append((self.source(where, height, width), (to, pl.ds(row, height), pl.ds(column, width))))

    def sum(self, role, wheres, to, width):
        to, row, column = to
        target = (to, pl.ds(row, self.rows), pl.ds(column, width))
        self.jobs[role].append(("sum", [self.source(w, self.rows, width) for w in wheres], [target], None))

    def gelu(self, role, chunk, wheres, out_where, hidden_to, grad_to, width):
        known = [entry[0] for entry in self.shared]
        if chunk not in known:
            self.shared.append((chunk, self.source(out_where, self.rows, width), hidden_to, width))
            known.append(chunk)
        targets = [(to, pl.ds(row, self.rows), pl.ds(column, width)) for to, row, column in grad_to]
        sources = [self.source(w, self.rows, width) for w in wheres]
        self.jobs[role].append(("gelu", sources, targets, known.index(chunk)))

    def run(self, outer, token):
        rows, shared, moves = self.rows, self.shared, self.moves
        n_in, n_out = len(self.operands), len(self.outputs)
        slots = max(len(shared), 1)
        widest = max([entry[3] for entry in shared], default=128)

        def kernel(outer_ref, *refs):
            ins, outs = refs[1 : 1 + n_in], refs[1 + n_in : 1 + n_in + n_out]
            token_ref, loaded, sems = refs[1 + n_in + n_out :]
            token_ref[...] = jnp.zeros_like(token_ref)
            counter = [0]

            def begin(source, target):
                handle = pltpu.make_async_copy(source, target, sems.at[counter[0]])
                counter[0] += 1
                handle.start()
                return handle

            def window(buffers, spot):
                place, rows_at, columns_at = spot
                return buffers[place].at[rows_at, columns_at]

            def read(spot):
                place, rows_at, columns_at = spot
                return ins[place][rows_at, columns_at]

            def write(spot, value):
                place, rows_at, columns_at = spot
                outs[place][rows_at, columns_at] = value

            def by_role(wanted_kind, do):
                for role, wanted in ((OUTER, 1), (INNER, 0)):
                    jobs = [job for job in self.jobs[role] if job[0] == wanted_kind]
                    if jobs:

                        @pl.when(outer_ref[0] == wanted)
                        def _():
                            for job in jobs:
                                do(*job[1:])

            def do_sum(sources, targets, _):
                value = read(sources[0])
                if len(sources) > 1:
                    value = narrow(sum((wide(read(s)) for s in sources[1:]), wide(value)))
                write(targets[0], value)

            def do_gelu(sources, targets, slot):
                width = shared[slot][3]
                pre_act = sum((wide(read(s)) for s in sources[1:]), wide(read(sources[0])))
                activation, pullback = jax.vjp(gelu_tanh, pre_act)
                outs[shared[slot][2]][...] = narrow(activation)
                grad = narrow(pullback(wide(loaded[slot, :, :width]))[0])
                for target in targets:
                    write(target, grad)

            loads = [
                begin(window(ins, entry[1]), loaded.at[slot, :, pl.ds(0, entry[3])])
                for slot, entry in enumerate(shared)
            ]
            pending = [begin(window(ins, source), window(outs, target)) for source, target in moves]
            by_role("sum", do_sum)
            for handle in loads:
                handle.wait()
            by_role("gelu", do_gelu)
            for handle in pending:
                handle.wait()

        def is_far(array):
            return any(array is known for known in self.far_arrays)

        operands = [
            pltpu.with_memory_space_constraint(array, pltpu.HBM) if is_far(array) else array for array in self.operands
        ]
        anywhere = pl.BlockSpec(memory_space=pl.ANY)
        results = pl.pallas_call(
            kernel,
            out_shape=self.outputs + [jax.ShapeDtypeStruct((8, 128), jnp.float32)],
            in_specs=[pl.BlockSpec(memory_space=pltpu.SMEM), anywhere]
            + [anywhere if is_far(x) or place in self.idle else VMEM for place, x in enumerate(self.operands)],
            out_specs=[VMEM] * (n_out + 1),
            scratch_shapes=[
                pltpu.VMEM((slots, rows, widest), jnp.bfloat16),
                pltpu.SemaphoreType.DMA((slots + len(moves),)),
            ],
            compiler_params=pltpu.CompilerParams(vmem_limit_bytes=12 * 2**20),
            cost_estimate=COST,
        )(outer, token, *operands)
        return results[:-1], results[-1]


COST = pl.CostEstimate(flops=10**10, bytes_accessed=1000, transcendentals=0)
COLUMNS = 256


def forward(near_tokens, far_tokens, near, far):
    rows, width = near_tokens.shape[0], near.shape[1]

    def kernel(near_tokens_ref, far_tokens_ref, near_ref, far_ref, out_ref):
        @pl.loop(0, width // COLUMNS)
        def _(j):
            columns = pl.ds(pl.multiple_of(j * COLUMNS, COLUMNS), COLUMNS)
            part = jnp.dot(near_tokens_ref[...], near_ref[:, columns], preferred_element_type=jnp.float32)
            part = part + jnp.dot(far_tokens_ref[...], far_ref[:, columns], preferred_element_type=jnp.float32)
            out_ref[:, columns] = narrow(part)

    return pl.pallas_call(
        kernel,
        out_shape=jax.ShapeDtypeStruct((rows, width), jnp.bfloat16),
        in_specs=[VMEM] * 4,
        out_specs=VMEM,
        compiler_params=pltpu.CompilerParams(vmem_limit_bytes=12 * 2**20),
        cost_estimate=COST,
    )(near_tokens, far_tokens, near, far)


def backward(grad_block, near, far, total):
    rows = grad_block.shape[0]
    depth = near.shape[0]
    contract = (((1,), (1,)), ((), ()))

    def kernel(grad_ref, near_ref, far_ref, *refs):
        olds, news = refs[:-2], refs[-2:]

        @pl.loop(0, depth // COLUMNS)
        def _(j):
            columns = pl.ds(pl.multiple_of(j * COLUMNS, COLUMNS), COLUMNS)
            for place, part_ref in enumerate((near_ref, far_ref)):
                term = lax.dot_general(
                    grad_ref[...], part_ref[columns, :], contract, preferred_element_type=jnp.float32
                )
                news[place][:, columns] = olds[place][:, columns] + term if olds else term

    olds = list(total or [])
    return pl.pallas_call(
        kernel,
        out_shape=[jax.ShapeDtypeStruct((rows, depth), jnp.float32)] * 2,
        in_specs=[VMEM] * (3 + len(olds)),
        out_specs=[VMEM] * 2,
        input_output_aliases={3: 0, 4: 1} if olds else {},
        compiler_params=pltpu.CompilerParams(vmem_limit_bytes=12 * 2**20),
        cost_estimate=COST,
    )(grad_block, near, far, *olds)


def schedule(groups):
    after = {"A": (None, 0), "B": ("A", LAG), "C": ("B", LAG), "I": ("B", LAG), "G": ("C", LAG), "T": ("I", LAG)}
    after.update({"M": ("G", LAG), "U": ("M", LAG), "Z": ("U", LAG)})
    chunks = sum(len(group) for group in groups)
    when = {}
    for c in range(chunks):
        for item, (before, lag) in after.items():
            when[c, item] = c if before is None else when[c, before] + lag
    for group in groups:
        for c in group:
            when[c, "Z"] = when[group[-1], "Z"]
    return when


def line_body(inputs, weight, grad_out):
    row, col, dep = (lax.axis_index(name) for name in ("row", "col", "dep"))
    mirrored = col >= 2
    outer = ((col == 0) | (col == 3)).astype(jnp.int32).reshape(1)
    swap_pairs = [(0, 1), (1, 0), (2, 3), (3, 2)]
    middle_pair = [(1, 2), (2, 1)]
    chip_pairs = [(0, 2), (2, 0), (1, 3), (3, 1)]
    core_pairs = [(0, 1), (1, 0), (2, 3), (3, 2)]

    depth, hidden_width = weight.shape
    rows = grad_out.shape[0]
    shares = [share for group in SHARES for share in group]
    unit = hidden_width // sum(shares)
    sizes = [unit * share for share in shares]
    starts = [sum(sizes[:c]) for c in range(len(sizes))]
    chunks = len(sizes)
    groups = []
    for group in SHARES:
        first = groups[-1][-1] + 1 if groups else 0
        groups.append(list(range(first, first + len(group))))
    widths = [sum(sizes[c] for c in group) for group in groups]
    when = schedule(groups)
    last = max(when.values())

    def block(array, b):
        return array[b * rows : (b + 1) * rows]

    other_in = lax.ppermute(inputs, "dep", [(0, 1), (1, 0)])
    tokens = jnp.concatenate(
        [jnp.where(dep == 0, inputs, other_in), jnp.where(dep == 0, other_in, inputs)], axis=0
    )
    tokens = jnp.concatenate([jnp.where(mirrored, block(tokens, 3 - b), block(tokens, b)) for b in range(4)], axis=0)
    near_tokens, far_tokens = (
        jnp.concatenate([lax.dynamic_slice_in_dim(tokens, (row ^ flip) * depth, depth, 1) for flip in pair], axis=1)
        for pair in ((0, 2), (1, 3))
    )

    token = jnp.zeros((8, 128), jnp.float32)
    from_chip, near_weight, far_weight = {}, {}, {}
    place = {}
    hidden, total = {}, None

    for tick in range(-AHEAD, last + 1):
        kernel = Tick(rows, [weight, grad_out])

        def now(item):
            return [c for c in range(chunks) if when[c, item] == tick]

        def starting(ahead):
            return [g for g, group in enumerate(groups) if group[0] - ahead == tick]

        for g in starting(0):
            product = forward(near_tokens, far_tokens, near_weight[g], far_weight[g])
            for c in groups[g]:
                for role in (OUTER, INNER):
                    for b in range(4):
                        place[role, c, b] = (product, b * rows, starts[c] - starts[groups[g][0]])

        to_inner = [(c, "A%d" % b) for c in now("A") for b in (1, 2, 3)] + [(c, "first") for c in now("G")]
        to_outer = [(c, "C0") for c in now("C")]
        for item, name in (("I", "second"), ("T", "third"), ("U", "fourth")):
            to_outer += [(c, name) for c in now(item)]
        across = [(c, name) for c in now("B") for name in ("R1", "R0")]
        across += [(c, "third") for c in now("I")] + [(c, "fourth") for c in now("M")]

        def spots(message):
            found, column = {}, 0
            for c, name in message:
                found[c, name] = column
                column += sizes[c]
            return found, column

        inner_spots, inner_width = spots(to_inner)
        outer_spots, outer_width = spots(to_outer)
        across_spots, across_width = spots(across)
        swap_width = max(inner_width, outer_width)
        swap = kernel.output((rows, swap_width)) if swap_width else None
        middle = kernel.output((rows, across_width)) if across_width else None
        early_out = {c: kernel.output((rows, sizes[c])) for c in now("I")}
        hidden_out = {c: kernel.output((rows, sizes[c])) for c in now("G")}

        for c in now("A"):
            for b in (1, 2, 3):
                kernel.sum(OUTER, [place[OUTER, c, b]], (swap, 0, inner_spots[c, "A%d" % b]), sizes[c])
        for c in now("B"):
            for b, name in ((2, "R1"), (3, "R0")):
                terms = [place[INNER, c, b], place[INNER, c, "A%d" % b]]
                kernel.sum(INNER, terms, (middle, 0, across_spots[c, name]), sizes[c])
        for c in now("C"):
            terms = [place[INNER, c, 0], place[INNER, c, "R0"]]
            kernel.sum(INNER, terms, (swap, 0, outer_spots[c, "C0"]), sizes[c])
        for c in now("I"):
            terms = [place[INNER, c, 1], place[INNER, c, "A1"], place[INNER, c, "R1"]]
            sent = [(swap, 0, outer_spots[c, "second"]), (middle, 0, across_spots[c, "third"])]
            kernel.gelu(INNER, (INNER, c), terms, (grad_out, 0, starts[c]), early_out[c], sent, sizes[c])
        for c in now("G"):
            terms = [place[OUTER, c, 0], place[OUTER, c, "C0"]]
            sent = [(swap, 0, inner_spots[c, "first"])]
            kernel.gelu(OUTER, (OUTER, c), terms, (grad_out, 0, starts[c]), hidden_out[c], sent, sizes[c])
            kernel.sum(INNER, [(hidden.pop((INNER, c)), 0, 0)], (hidden_out[c], 0, 0), sizes[c])
        for c in now("M"):
            kernel.sum(INNER, [place[INNER, c, "first"]], (middle, 0, across_spots[c, "fourth"]), sizes[c])
        for item, name in (("T", "third"), ("U", "fourth")):
            for c in now(item):
                kernel.sum(INNER, [place[INNER, c, name]], (swap, 0, outer_spots[c, name]), sizes[c])
        blocks = {}
        for g, group in enumerate(groups):
            if when[group[0], "Z"] != tick:
                continue
            blocks[g] = kernel.output((4 * rows, widths[g]))
            for c in group:
                column = starts[c] - starts[group[0]]
                for role, names in ((OUTER, ("own", "second")), (INNER, ("first", "own"))):
                    for b, name in enumerate(names + ("third", "fourth")):
                        kernel.sum(role, [place[role, c, name]], (blocks[g], b * rows, column), sizes[c])

        asked = {g: kernel.output((depth, widths[g])) for g in starting(AHEAD)}
        for g, to in asked.items():
            kernel.move((weight, 0, starts[groups[g][0]]), (to, 0, 0), depth, widths[g])
        joined = {g: kernel.output((2 * depth, widths[g])) for g in starting(JOIN)}
        for g, to in joined.items():
            kernel.move((weight, 0, starts[groups[g][0]]), (to, 0, 0), depth, widths[g])
            kernel.move((from_chip[g], 0, 0), (to, depth, 0), depth, widths[g])
        for array in total or ():
            kernel.after(array)
        if not kernel.outputs:
            continue

        outs, token = kernel.run(outer, token)

        for c, to in early_out.items():
            hidden[INNER, c] = outs[to]
        for c, to in hidden_out.items():
            hidden[c] = outs[to]
        if swap is not None:
            arrived = lax.ppermute(outs[swap], "col", swap_pairs)
            for role, found in ((INNER, inner_spots), (OUTER, outer_spots)):
                for (c, name), column in found.items():
                    place[role, c, name] = (arrived, 0, column)
        if middle is not None:
            arrived = lax.ppermute(outs[middle], "col", middle_pair)
            for (c, name), column in across_spots.items():
                place[INNER, c, name] = (arrived, 0, column)
        for c in now("G"):
            place[OUTER, c, "own"] = (outs[swap], 0, inner_spots[c, "first"])
        for c in now("I"):
            place[INNER, c, "own"] = (outs[middle], 0, across_spots[c, "third"])
        for g, to in asked.items():
            from_chip[g] = lax.ppermute(outs[to], "row", chip_pairs)
        for g, to in joined.items():
            near_weight[g] = outs[to]
            far_weight[g] = lax.ppermute(outs[to], "row", core_pairs)
        for g, to in blocks.items():
            total = backward(outs[to], near_weight.pop(g), far_weight.pop(g), total)

    half = 2 * rows
    other_half = jnp.where(mirrored, dep, 1 - dep) * half
    own_half = jnp.where(mirrored, 1 - dep, dep) * half
    result = []
    for part in total:
        sent = lax.ppermute(narrow(lax.dynamic_slice_in_dim(part, other_half, half, 0)), "dep", [(0, 1), (1, 0)])
        own = narrow(lax.dynamic_slice_in_dim(part, own_half, half, 0))
        result.append(narrow(wide(sent) + wide(own)))
    result = jnp.concatenate(result, axis=1)
    result = jnp.where(mirrored, jnp.concatenate([result[rows:], result[:rows]], axis=0), result)
    place_of = jnp.array([0, 2, 1, 3], jnp.int32)
    result = jnp.concatenate(
        [lax.dynamic_slice_in_dim(result, place_of[row ^ j] * depth, depth, 1) for j in range(4)], axis=1
    )
    return (jnp.concatenate([hidden[c] for c in range(chunks)], axis=1), result)


def solution(mesh):
    sizes = tuple(mesh.shape[name] for name in ("row", "col", "dep"))
    body = line_body if sizes == (4, 4, 2) else plain_body
    placed = (P(("row", "dep"), "col"), P(("col", "row"), "dep"), P(("row", "col"), "dep"))
    return jax.shard_map(
        body,
        mesh=mesh,
        in_specs=placed,
        out_specs=(P(("row", "col"), "dep"), P(("row", "dep"), "col")),
        check_vma=False,
    )
```

```python
import jax
import jax.numpy as jnp
from jax import lax
from jax.experimental import pallas as pl
from jax.experimental.pallas import tpu as pltpu
from jax.sharding import PartitionSpec as P

SHARES = ((1,), (1,)) + ((2,),) * 19 + ((1, 1),) * 2 + ((1,),) * 4
LAG = 2
AHEAD, JOIN = 4, 2
OUTER, INNER = "outer", "inner"


def gelu_tanh(values):
    return jax.nn.gelu(values, approximate=True)


def wide(values):
    return values.astype(jnp.float32)


def narrow(values):
    return values.astype(jnp.bfloat16)


def plain_body(inputs, weight, grad_out):
    block_in = lax.all_gather(inputs, "dep", axis=0, tiled=True)
    full_weight = lax.all_gather(weight, "row", axis=0, tiled=True)
    partial_sum = jnp.dot(block_in, full_weight, preferred_element_type=jnp.float32)
    pre_act = wide(lax.psum_scatter(narrow(partial_sum), "col", scatter_dimension=0, tiled=True))
    activation, pullback = jax.vjp(gelu_tanh, pre_act)
    grad_local = narrow(pullback(wide(grad_out))[0])
    grad_block = lax.all_gather(grad_local, "col", axis=0, tiled=True)
    partial_grad = lax.dot_general(
        grad_block, full_weight, (((1,), (1,)), ((), ())), preferred_element_type=jnp.float32
    )
    grad_inputs = lax.psum_scatter(narrow(partial_grad), "dep", scatter_dimension=0, tiled=True)
    return (narrow(activation), grad_inputs)


VMEM = pl.BlockSpec(memory_space=pltpu.VMEM)


class Tick:
    def __init__(self, rows, far_arrays):
        self.rows, self.far_arrays = rows, far_arrays
        self.operands, self.outputs, self.idle = [], [], set()
        self.moves, self.shared = [], []
        self.jobs = {OUTER: [], INNER: []}

    def operand(self, array):
        for place, known in enumerate(self.operands):
            if known is array:
                return place
        self.operands.append(array)
        return len(self.operands) - 1

    def output(self, shape):
        self.outputs.append(jax.ShapeDtypeStruct(shape, jnp.bfloat16))
        return len(self.outputs) - 1

    def after(self, array):
        self.idle.add(self.operand(array))

    def source(self, where, height, width):
        array, row, column = where
        return (self.operand(array), pl.ds(row, height), pl.ds(column, width))

    def move(self, where, to, height, width):
        to, row, column = to
        self.moves.append((self.source(where, height, width), (to, pl.ds(row, height), pl.ds(column, width))))

    def sum(self, role, wheres, to, width):
        to, row, column = to
        target = (to, pl.ds(row, self.rows), pl.ds(column, width))
        self.jobs[role].append(("sum", [self.source(w, self.rows, width) for w in wheres], [target], None))

    def gelu(self, role, chunk, wheres, out_where, hidden_to, grad_to, width):
        known = [entry[0] for entry in self.shared]
        if chunk not in known:
            self.shared.append((chunk, self.source(out_where, self.rows, width), hidden_to, width))
            known.append(chunk)
        targets = [(to, pl.ds(row, self.rows), pl.ds(column, width)) for to, row, column in grad_to]
        sources = [self.source(w, self.rows, width) for w in wheres]
        self.jobs[role].append(("gelu", sources, targets, known.index(chunk)))

    def run(self, outer, token):
        rows, shared, moves = self.rows, self.shared, self.moves
        n_in, n_out = len(self.operands), len(self.outputs)
        slots = max(len(shared), 1)
        widest = max([entry[3] for entry in shared], default=128)

        def kernel(outer_ref, *refs):
            ins, outs = refs[1 : 1 + n_in], refs[1 + n_in : 1 + n_in + n_out]
            token_ref, loaded, sems = refs[1 + n_in + n_out :]
            token_ref[...] = jnp.zeros_like(token_ref)
            counter = [0]

            def begin(source, target):
                handle = pltpu.make_async_copy(source, target, sems.at[counter[0]])
                counter[0] += 1
                handle.start()
                return handle

            def window(buffers, spot):
                place, rows_at, columns_at = spot
                return buffers[place].at[rows_at, columns_at]

            def read(spot):
                place, rows_at, columns_at = spot
                return ins[place][rows_at, columns_at]

            def write(spot, value):
                place, rows_at, columns_at = spot
                outs[place][rows_at, columns_at] = value

            def by_role(wanted_kind, do):
                for role, wanted in ((OUTER, 1), (INNER, 0)):
                    jobs = [job for job in self.jobs[role] if job[0] == wanted_kind]
                    if jobs:

                        @pl.when(outer_ref[0] == wanted)
                        def _():
                            for job in jobs:
                                do(*job[1:])

            def do_sum(sources, targets, _):
                value = read(sources[0])
                if len(sources) > 1:
                    value = narrow(sum((wide(read(s)) for s in sources[1:]), wide(value)))
                write(targets[0], value)

            def do_gelu(sources, targets, slot):
                width = shared[slot][3]
                pre_act = sum((wide(read(s)) for s in sources[1:]), wide(read(sources[0])))
                activation, pullback = jax.vjp(gelu_tanh, pre_act)
                outs[shared[slot][2]][...] = narrow(activation)
                grad = narrow(pullback(wide(loaded[slot, :, :width]))[0])
                for target in targets:
                    write(target, grad)

            loads = [
                begin(window(ins, entry[1]), loaded.at[slot, :, pl.ds(0, entry[3])])
                for slot, entry in enumerate(shared)
            ]
            pending = [begin(window(ins, source), window(outs, target)) for source, target in moves]
            by_role("sum", do_sum)
            for handle in loads:
                handle.wait()
            by_role("gelu", do_gelu)
            for handle in pending:
                handle.wait()

        def is_far(array):
            return any(array is known for known in self.far_arrays)

        operands = [
            pltpu.with_memory_space_constraint(array, pltpu.HBM) if is_far(array) else array for array in self.operands
        ]
        anywhere = pl.BlockSpec(memory_space=pl.ANY)
        results = pl.pallas_call(
            kernel,
            out_shape=self.outputs + [jax.ShapeDtypeStruct((8, 128), jnp.float32)],
            in_specs=[pl.BlockSpec(memory_space=pltpu.SMEM), anywhere]
            + [anywhere if is_far(x) or place in self.idle else VMEM for place, x in enumerate(self.operands)],
            out_specs=[VMEM] * (n_out + 1),
            scratch_shapes=[
                pltpu.VMEM((slots, rows, widest), jnp.bfloat16),
                pltpu.SemaphoreType.DMA((slots + len(moves),)),
            ],
            compiler_params=pltpu.CompilerParams(vmem_limit_bytes=12 * 2**20),
            cost_estimate=COST,
        )(outer, token, *operands)
        return results[:-1], results[-1]


COST = pl.CostEstimate(flops=10**10, bytes_accessed=1000, transcendentals=0)
COLUMNS = 256


def forward(near_tokens, far_tokens, near, far):
    rows, width = near_tokens.shape[0], near.shape[1]

    def kernel(near_tokens_ref, far_tokens_ref, near_ref, far_ref, out_ref):
        @pl.loop(0, width // COLUMNS)
        def _(j):
            columns = pl.ds(pl.multiple_of(j * COLUMNS, COLUMNS), COLUMNS)
            part = jnp.dot(near_tokens_ref[...], near_ref[:, columns], preferred_element_type=jnp.float32)
            part = part + jnp.dot(far_tokens_ref[...], far_ref[:, columns], preferred_element_type=jnp.float32)
            out_ref[:, columns] = narrow(part)

    return pl.pallas_call(
        kernel,
        out_shape=jax.ShapeDtypeStruct((rows, width), jnp.bfloat16),
        in_specs=[VMEM] * 4,
        out_specs=VMEM,
        compiler_params=pltpu.CompilerParams(vmem_limit_bytes=12 * 2**20),
        cost_estimate=COST,
    )(near_tokens, far_tokens, near, far)


def backward(grad_block, near, far, total):
    rows = grad_block.shape[0]
    depth = near.shape[0]
    contract = (((1,), (1,)), ((), ()))

    def kernel(grad_ref, near_ref, far_ref, *refs):
        olds, news = refs[:-2], refs[-2:]

        @pl.loop(0, depth // COLUMNS)
        def _(j):
            columns = pl.ds(pl.multiple_of(j * COLUMNS, COLUMNS), COLUMNS)
            for place, part_ref in enumerate((near_ref, far_ref)):
                term = lax.dot_general(
                    grad_ref[...], part_ref[columns, :], contract, preferred_element_type=jnp.float32
                )
                news[place][:, columns] = olds[place][:, columns] + term if olds else term

    olds = list(total or [])
    return pl.pallas_call(
        kernel,
        out_shape=[jax.ShapeDtypeStruct((rows, depth), jnp.float32)] * 2,
        in_specs=[VMEM] * (3 + len(olds)),
        out_specs=[VMEM] * 2,
        input_output_aliases={3: 0, 4: 1} if olds else {},
        compiler_params=pltpu.CompilerParams(vmem_limit_bytes=12 * 2**20),
        cost_estimate=COST,
    )(grad_block, near, far, *olds)


def schedule(groups):
    after = {"A": (None, 0), "B": ("A", LAG), "C": ("B", LAG), "I": ("B", LAG), "G": ("C", LAG), "T": ("I", LAG)}
    after.update({"M": ("G", LAG), "U": ("M", LAG), "Z": ("U", LAG)})
    chunks = sum(len(group) for group in groups)
    when = {}
    for c in range(chunks):
        for item, (before, lag) in after.items():
            when[c, item] = c if before is None else when[c, before] + lag
    for group in groups:
        for c in group:
            when[c, "Z"] = when[group[-1], "Z"]
    return when


def line_body(inputs, weight, grad_out):
    row, col, dep = (lax.axis_index(name) for name in ("row", "col", "dep"))
    mirrored = col >= 2
    outer = ((col == 0) | (col == 3)).astype(jnp.int32).reshape(1)
    swap_pairs = [(0, 1), (1, 0), (2, 3), (3, 2)]
    middle_pair = [(1, 2), (2, 1)]
    chip_pairs = [(0, 2), (2, 0), (1, 3), (3, 1)]
    core_pairs = [(0, 1), (1, 0), (2, 3), (3, 2)]

    depth, hidden_width = weight.shape
    rows = grad_out.shape[0]
    shares = [share for group in SHARES for share in group]
    unit = hidden_width // sum(shares)
    sizes = [unit * share for share in shares]
    starts = [sum(sizes[:c]) for c in range(len(sizes))]
    chunks = len(sizes)
    groups = []
    for group in SHARES:
        first = groups[-1][-1] + 1 if groups else 0
        groups.append(list(range(first, first + len(group))))
    widths = [sum(sizes[c] for c in group) for group in groups]
    when = schedule(groups)
    last = max(when.values())

    def block(array, b):
        return array[b * rows : (b + 1) * rows]

    other_in = lax.ppermute(inputs, "dep", [(0, 1), (1, 0)])
    tokens = jnp.concatenate(
        [jnp.where(dep == 0, inputs, other_in), jnp.where(dep == 0, other_in, inputs)], axis=0
    )
    tokens = jnp.concatenate([jnp.where(mirrored, block(tokens, 3 - b), block(tokens, b)) for b in range(4)], axis=0)
    near_tokens, far_tokens = (
        jnp.concatenate([lax.dynamic_slice_in_dim(tokens, (row ^ flip) * depth, depth, 1) for flip in pair], axis=1)
        for pair in ((0, 2), (1, 3))
    )

    token = jnp.zeros((8, 128), jnp.float32)
    from_chip, near_weight, far_weight = {}, {}, {}
    place = {}
    hidden, total = {}, None

    for tick in range(-AHEAD, last + 1):
        kernel = Tick(rows, [weight, grad_out])

        def now(item):
            return [c for c in range(chunks) if when[c, item] == tick]

        def starting(ahead):
            return [g for g, group in enumerate(groups) if group[0] - ahead == tick]

        for g in starting(0):
            product = forward(near_tokens, far_tokens, near_weight[g], far_weight[g])
            for c in groups[g]:
                for role in (OUTER, INNER):
                    for b in range(4):
                        place[role, c, b] = (product, b * rows, starts[c] - starts[groups[g][0]])

        to_inner = [(c, "A%d" % b) for c in now("A") for b in (1, 2, 3)] + [(c, "first") for c in now("G")]
        to_outer = [(c, "C0") for c in now("C")]
        for item, name in (("I", "second"), ("T", "third"), ("U", "fourth")):
            to_outer += [(c, name) for c in now(item)]
        across = [(c, name) for c in now("B") for name in ("R1", "R0")]
        across += [(c, "third") for c in now("I")] + [(c, "fourth") for c in now("M")]

        def spots(message):
            found, column = {}, 0
            for c, name in message:
                found[c, name] = column
                column += sizes[c]
            return found, column

        inner_spots, inner_width = spots(to_inner)
        outer_spots, outer_width = spots(to_outer)
        across_spots, across_width = spots(across)
        swap_width = max(inner_width, outer_width)
        swap = kernel.output((rows, swap_width)) if swap_width else None
        middle = kernel.output((rows, across_width)) if across_width else None
        early_out = {c: kernel.output((rows, sizes[c])) for c in now("I")}
        hidden_out = {c: kernel.output((rows, sizes[c])) for c in now("G")}

        for c in now("A"):
            for b in (1, 2, 3):
                kernel.sum(OUTER, [place[OUTER, c, b]], (swap, 0, inner_spots[c, "A%d" % b]), sizes[c])
        for c in now("B"):
            for b, name in ((2, "R1"), (3, "R0")):
                terms = [place[INNER, c, b], place[INNER, c, "A%d" % b]]
                kernel.sum(INNER, terms, (middle, 0, across_spots[c, name]), sizes[c])
        for c in now("C"):
            terms = [place[INNER, c, 0], place[INNER, c, "R0"]]
            kernel.sum(INNER, terms, (swap, 0, outer_spots[c, "C0"]), sizes[c])
        for c in now("I"):
            terms = [place[INNER, c, 1], place[INNER, c, "A1"], place[INNER, c, "R1"]]
            sent = [(swap, 0, outer_spots[c, "second"]), (middle, 0, across_spots[c, "third"])]
            kernel.gelu(INNER, (INNER, c), terms, (grad_out, 0, starts[c]), early_out[c], sent, sizes[c])
        for c in now("G"):
            terms = [place[OUTER, c, 0], place[OUTER, c, "C0"]]
            sent = [(swap, 0, inner_spots[c, "first"])]
            kernel.gelu(OUTER, (OUTER, c), terms, (grad_out, 0, starts[c]), hidden_out[c], sent, sizes[c])
            kernel.sum(INNER, [(hidden.pop((INNER, c)), 0, 0)], (hidden_out[c], 0, 0), sizes[c])
        for c in now("M"):
            kernel.sum(INNER, [place[INNER, c, "first"]], (middle, 0, across_spots[c, "fourth"]), sizes[c])
        for item, name in (("T", "third"), ("U", "fourth")):
            for c in now(item):
                kernel.sum(INNER, [place[INNER, c, name]], (swap, 0, outer_spots[c, name]), sizes[c])
        blocks = {}
        for g, group in enumerate(groups):
            if when[group[0], "Z"] != tick:
                continue
            blocks[g] = kernel.output((4 * rows, widths[g]))
            for c in group:
                column = starts[c] - starts[group[0]]
                for role, names in ((OUTER, ("own", "second")), (INNER, ("first", "own"))):
                    for b, name in enumerate(names + ("third", "fourth")):
                        kernel.sum(role, [place[role, c, name]], (blocks[g], b * rows, column), sizes[c])

        asked = {g: kernel.output((depth, widths[g])) for g in starting(AHEAD)}
        for g, to in asked.items():
            kernel.move((weight, 0, starts[groups[g][0]]), (to, 0, 0), depth, widths[g])
        joined = {g: kernel.output((2 * depth, widths[g])) for g in starting(JOIN)}
        for g, to in joined.items():
            kernel.move((weight, 0, starts[groups[g][0]]), (to, 0, 0), depth, widths[g])
            kernel.move((from_chip[g], 0, 0), (to, depth, 0), depth, widths[g])
        for array in total or ():
            kernel.after(array)
        if not kernel.outputs:
            continue

        outs, token = kernel.run(outer, token)

        for c, to in early_out.items():
            hidden[INNER, c] = outs[to]
        for c, to in hidden_out.items():
            hidden[c] = outs[to]
        if swap is not None:
            arrived = lax.ppermute(outs[swap], "col", swap_pairs)
            for role, found in ((INNER, inner_spots), (OUTER, outer_spots)):
                for (c, name), column in found.items():
                    place[role, c, name] = (arrived, 0, column)
        if middle is not None:
            arrived = lax.ppermute(outs[middle], "col", middle_pair)
            for (c, name), column in across_spots.items():
                place[INNER, c, name] = (arrived, 0, column)
        for c in now("G"):
            place[OUTER, c, "own"] = (outs[swap], 0, inner_spots[c, "first"])
        for c in now("I"):
            place[INNER, c, "own"] = (outs[middle], 0, across_spots[c, "third"])
        for g, to in asked.items():
            from_chip[g] = lax.ppermute(outs[to], "row", chip_pairs)
        for g, to in joined.items():
            near_weight[g] = outs[to]
            far_weight[g] = lax.ppermute(outs[to], "row", core_pairs)
        for g, to in blocks.items():
            total = backward(outs[to], near_weight.pop(g), far_weight.pop(g), total)

    half = 2 * rows
    other_half = jnp.where(mirrored, dep, 1 - dep) * half
    own_half = jnp.where(mirrored, 1 - dep, dep) * half
    result = []
    for part in total:
        sent = lax.ppermute(narrow(lax.dynamic_slice_in_dim(part, other_half, half, 0)), "dep", [(0, 1), (1, 0)])
        own = narrow(lax.dynamic_slice_in_dim(part, own_half, half, 0))
        result.append(narrow(wide(sent) + wide(own)))
    result = jnp.concatenate(result, axis=1)
    result = jnp.where(mirrored, jnp.concatenate([result[rows:], result[:rows]], axis=0), result)
    place_of = jnp.array([0, 2, 1, 3], jnp.int32)
    result = jnp.concatenate(
        [lax.dynamic_slice_in_dim(result, place_of[row ^ j] * depth, depth, 1) for j in range(4)], axis=1
    )
    return (jnp.concatenate([hidden[c] for c in range(chunks)], axis=1), result)


def solution(mesh):
    sizes = tuple(mesh.shape[name] for name in ("row", "col", "dep"))
    body = line_body if sizes == (4, 4, 2) else plain_body
    placed = (P(("row", "dep"), "col"), P(("col", "row"), "dep"), P(("row", "col"), "dep"))
    return jax.shard_map(
        body,
        mesh=mesh,
        in_specs=placed,
        out_specs=(P(("row", "col"), "dep"), P(("row", "dep"), "col")),
        check_vma=False,
    )
```
